32 devices in a mesh: section: 4 (over y, x), grp: 4 (over z), cent: 2 (over core).
Axes of the slice: x: 2, y: 2, z: 4, core: 2. Of those that a mesh axis runs over, the one named last changes fastest.
Arguments:
- latents: bfloat16 [768, 1024], P(('section', 'grp', 'cent')), may hold values from -27 to 27
- valid_mask: int32 [768], P(('section', 'grp', 'cent')), may hold values from 0 to 1, as said below
- centroids: float32 [65536, 1024], P(('section', 'cent')), may hold values from -12 to 12
Outputs:
- refreshed: float32 [65536, 1024], P(('section', 'cent'))
The draws below stay inside these ranges and needn't reach their ends.
Inputs may be any that keep to these rules, and one draw needn't show every extreme that they name: `valid_mask`: each device's block of 24 frames has its valid frames first; a block has at least 6 and at most 18 valid frames, and some block has exactly 18.
All inputs are finite; a program needn't handle non-finite values.
Results may differ from the reference program's by a relative error of at most 0.0044.
Values may be sent and summed in bfloat16 or wider, within the bound.
No kernel may reach another device: no remote copies, remote signals or barrier semaphores. Data moves between devices by JAX's collectives and lax.ppermute only.
A program may use at most 192 MiB of HBM per device.

```python
import math
import jax
import jax.numpy as jnp
from jax import lax

W = 1024
K = 65536
FR_DEV = 24
VMAX = 18
FRAMES = 768


def draw_common(key):
    base_noise = jnp.clip(jax.random.normal(jax.random.fold_in(key, 11), (K, W), jnp.float32), -5.0, 5.0)
    rise_factor = 1.0 + 0.15 * jnp.arange(K, dtype=jnp.float32) / K
    centers = base_noise * rise_factor[:, None]
    return centers


def draw_centroids(key, part):
    centers = draw_common(key)
    return centers


def draw_latents(key, part):
    noise = jnp.clip(jax.random.normal(jax.random.fold_in(key, 21), (FRAMES, W), jnp.float32), -5.0, 5.0)
    return noise.astype(jnp.bfloat16)


def draw_valid_mask(key, part):
    blocks = FRAMES // FR_DEV
    lengths = jax.random.randint(jax.random.fold_in(key, 31), (blocks,), FR_DEV // 4, VMAX + 1)
    fullest = jax.random.randint(jax.random.fold_in(key, 32), (), 0, blocks)
    lengths = lengths.at[fullest].set(VMAX)
    positions = jnp.arange(FR_DEV)
    return (positions[None, :] < lengths[:, None]).astype(jnp.int32).reshape(FRAMES)


def setup_inputs(seed: int = 0) -> dict:
    splits = jax.random.split(jax.random.key(seed), 4)
    return {
        "latents": draw_latents(jax.random.fold_in(splits[3], 71), 0),
        "valid_mask": draw_valid_mask(jax.random.fold_in(splits[3], 71), 0),
        "centroids": draw_centroids(jax.random.fold_in(splits[3], 71), 0),
    }


prior_weight = 0.05

def reference(latents, valid_mask, centroids):
    inverse_temp = 3.0 / math.sqrt(W)
    cent_low = centroids.astype(jnp.bfloat16)
    block_size = min(K, 4096)
    num_blocks = K // block_size
    cent_blocks = cent_low.reshape(num_blocks, block_size, W)

    def score_block(block_cent):
        return jnp.dot(latents, block_cent.T, preferred_element_type=jnp.float32) * inverse_temp
    scores = lax.map(score_block, cent_blocks)
    row_max = lax.optimization_barrier(jnp.max(scores, axis=(0, 2)))
    row_total = lax.optimization_barrier(jnp.sum(jnp.exp(scores - row_max[None, :, None]), axis=(0, 2)))
    keep_mask = valid_mask.astype(jnp.float32)

    def update_block(pieces):
        block_scores, block_cent = pieces
        weights = (keep_mask[:, None] * jnp.exp(block_scores - row_max[:, None]) / row_total[:, None]).astype(jnp.bfloat16)
        center_sums = lax.dot_general(weights, latents, (((0,), (0,)), ((), ())), preferred_element_type=jnp.float32)
        soft_counts = lax.optimization_barrier(jnp.sum(weights, axis=0, dtype=jnp.float32))
        return (center_sums + prior_weight * block_cent) / (soft_counts + prior_weight)[:, None]
    refreshed = lax.map(update_block, (scores, centroids.reshape(num_blocks, block_size, W)))
    return refreshed.reshape(K, W)
```

```python
import functools
import math

import jax
import jax.numpy as jnp
from jax import lax
from jax.experimental import pallas as pl
from jax.experimental.pallas import tpu as pltpu
from jax.sharding import PartitionSpec as P

VMAX = 18
LANES = 128
ROWS = 16
f32, bf16 = jnp.float32, jnp.bfloat16

prior_weight = 0.05


def pack_body(axes, lat_ref, mask_ref, out_ref):
    width = lat_ref.shape[1]
    rows = lat_ref[...].astype(f32)
    fold = width // LANES
    pieces = [
        rows[r : r + 1, j * LANES : (j + 1) * LANES] for r in range(ROWS, VMAX) for j in range(fold)
    ]
    count = jnp.sum(mask_ref[...].astype(f32), axis=1, keepdims=True)
    block = jnp.int32(0)
    for name, size in axes:
        block = block * size + lax.axis_index(name)
    lane = lax.broadcasted_iota(jnp.int32, (ROWS, LANES), 1)
    tail = jnp.where(lane == 0, count, jnp.where(lane == 1, block.astype(f32), 0.0))
    out_ref[:, :width] = rows[:ROWS].astype(bf16)
    out_ref[:, width : width + LANES] = jnp.concatenate(pieces, axis=0).astype(bf16)
    out_ref[:, width + LANES :] = tail.astype(bf16)


def scores_body(k, cb, sizes, c_ref, *refs):
    n_in = len(refs) - 8
    packed = refs[:n_in]
    fr_ref, e_ref, mb_ref, st_ref, n_ref, all_ref, ext_ref, meta_ref = refs[n_in:]
    cents, width = c_ref.shape
    frames = fr_ref.shape[0]
    steps = cents // cb

    at = 0
    for part in packed:
        for i in range(part.shape[0]):
            all_ref[at : at + ROWS, :] = part[i, :, :width]
            ext_ref[at : at + ROWS, :] = part[i, :, width : width + LANES].astype(f32)
            meta_ref[at : at + ROWS, :] = part[i, :, width + LANES :].astype(f32)
            at += ROWS
    blocks = at // ROWS
    meta = meta_ref[pl.ds(0, blocks, stride=ROWS), :]
    count, number = meta[:, 0:1], meta[:, 1:2]
    total = jnp.sum(count)
    n_ref[0] = total.astype(jnp.int32)

    def place(rows, block_of, row_of):
        block = lax.broadcasted_iota(jnp.int32, (blocks, rows), 0)
        r = lax.broadcasted_iota(jnp.int32, (blocks, rows), 1)
        mine = block == block_of(r)
        length = jnp.sum(jnp.where(mine, count, 0.0), axis=0, keepdims=True)
        own = jnp.sum(jnp.where(mine, number, 0.0), axis=0, keepdims=True)
        before = jnp.sum(jnp.where(number < own, count, 0.0), axis=0, keepdims=True)
        row = row_of(lax.broadcasted_iota(jnp.int32, (1, rows), 1)).astype(f32)
        return jnp.where(row < length, before + row, -1.0)

    def one_hot(to):
        p = lax.broadcasted_iota(jnp.int32, (frames, to.shape[1]), 0).astype(f32)
        return jnp.where(p == to, 1.0, 0.0).astype(bf16)

    extra = VMAX - ROWS
    fold = width // LANES
    main_to = place(at, lambda r: r // ROWS, lambda r: r % ROWS)
    extra_to = place(extra * blocks, lambda r: r % blocks, lambda r: ROWS + r // blocks)
    extra_rows = jnp.concatenate(
        [
            jnp.concatenate(
                [ext_ref[pl.ds(r * fold + j, blocks, stride=ROWS), :] for j in range(fold)], axis=1
            )
            for r in range(extra)
        ],
        axis=0,
    ).astype(bf16)
    ordered = lax.dot_general(
        one_hot(main_to), all_ref[...], (((1,), (0,)), ((), ())), preferred_element_type=f32
    ) + lax.dot_general(
        one_hot(extra_to), extra_rows, (((1,), (0,)), ((), ())), preferred_element_type=f32
    )
    fr_ref[...] = ordered.astype(bf16)

    def run(size):
        st_ref[...] = jnp.zeros_like(st_ref)

        def step(b, carry):
            top, tot = carry
            rows = pl.ds(pl.multiple_of(b * cb, cb), cb)
            raw = lax.dot_general(
                c_ref[rows, :].astype(bf16),
                fr_ref[:size, :],
                (((1,), (1,)), ((), ())),
                preferred_element_type=f32,
            )
            m = jnp.max(raw, axis=0, keepdims=True)
            e = jnp.exp2((raw - m) * k)
            e_ref[rows, :size] = e.astype(bf16)
            mb_ref[b, :, :size] = jnp.broadcast_to(m, (8, size))
            new = jnp.maximum(top, m)
            tot = tot * jnp.exp2((top - new) * k) + jnp.sum(e, axis=0, keepdims=True) * jnp.exp2(
                (m - new) * k
            )
            return new, tot

        top, tot = lax.fori_loop(
            0, steps, step, (jnp.full((1, size), -1e30, f32), jnp.zeros((1, size), f32)), unroll=2
        )
        st_ref[0:1, :size] = top
        st_ref[1:2, :size] = tot

    for i, size in enumerate(sizes):
        over = total > (sizes[i - 1] if i else -1)
        within = total <= size if size < frames else True
        pl.when(jnp.logical_and(over, within))(functools.partial(run, size))


def refresh_body(k, cb, sizes, c_ref, fr_ref, e_ref, mb_ref, n_ref, *refs):
    stats, (o_ref, out_buf, sem) = refs[:-3], refs[-3:]
    cents, width = c_ref.shape
    frames = fr_ref.shape[0]
    steps = cents // cb
    total = n_ref[0]

    def run(size):
        top = functools.reduce(jnp.maximum, [s[0:1, :size] for s in stats])
        denom = functools.reduce(
            jnp.add, [s[1:2, :size] * jnp.exp2((s[0:1, :size] - top) * k) for s in stats]
        )
        valid = lax.broadcasted_iota(jnp.int32, (1, size), 1) < total
        keep = jnp.where(valid, 1.0 / denom, 0.0)

        def out_copy(slot, rows):
            return pltpu.make_async_copy(out_buf.at[slot], o_ref.at[rows, :], sem.at[slot])

        def step(b, _):
            rows = pl.ds(pl.multiple_of(b * cb, cb), cb)
            scale = jnp.exp2((mb_ref[b * cb // mb_rows, 0:1, :size] - top) * k) * keep
            w = (e_ref[rows, :size].astype(f32) * scale).astype(bf16)
            sums = lax.dot_general(
                w, fr_ref[:size, :], (((1,), (0,)), ((), ())), preferred_element_type=f32
            )
            soft = jnp.sum(w.astype(f32), axis=1, keepdims=True)
            slot = lax.rem(b, 2)

            @pl.when(b >= 2)
            def _():
                out_copy(slot, rows).wait()

            out_buf[slot] = (sums + prior_weight * c_ref[rows, :]) * (1.0 / (soft + prior_weight))
            out_copy(slot, rows).start()
            return 0

        mb_rows = cents // mb_ref.shape[0]
        lax.fori_loop(0, steps, step, 0)
        for slot in range(2):
            out_copy(slot, pl.ds(0, cb)).wait()

    for i, size in enumerate(sizes):
        over = total > (sizes[i - 1] if i else -1)
        within = total <= size if size < frames else True
        pl.when(jnp.logical_and(over, within))(functools.partial(run, size))


VMEM = pl.BlockSpec(memory_space=pltpu.VMEM)
SMEM = pl.BlockSpec(memory_space=pltpu.SMEM)


def exchange(x, axis, size):
    return [lax.ppermute(x, axis, [(i, i ^ d) for i in range(size)]) for d in range(1, size)]


def fast(sizes, latents, valid_mask, centroids):
    cents, width = centroids.shape
    k = 3.0 / math.sqrt(width) * math.log2(math.e)
    section, grp, cent = sizes["section"], sizes["grp"], sizes["cent"]
    blocks = section * grp * cent
    frames = -(-blocks * VMAX // LANES) * LANES
    batch = [s for s in (frames * 4 // 5 // LANES * LANES,) if s] + [frames]
    cb_a, cb_b = min(512, cents), min(256, cents)

    packed = pl.pallas_call(
        functools.partial(pack_body, (("section", section), ("grp", grp), ("cent", cent))),
        in_specs=[VMEM, VMEM],
        out_specs=VMEM,
        out_shape=jax.ShapeDtypeStruct((ROWS, width + 2 * LANES), bf16),
        name="pack",
    )(latents, valid_mask[None, :])

    column = jnp.stack([packed] + exchange(packed, "grp", grp))
    half = [column] + exchange(column, "section", section)
    parts = half + [x for h in half for x in exchange(h, "cent", cent)]

    held = pltpu.with_memory_space_constraint(centroids, pltpu.VMEM)
    steps = cents // cb_a
    frame_rows, e, mb, stats, total = pl.pallas_call(
        functools.partial(scores_body, k, cb_a, batch),
        in_specs=[VMEM] * (1 + len(parts)),
        out_specs=[VMEM] * 4 + [SMEM],
        out_shape=[
            pltpu.VMEM((frames, width), bf16),
            pltpu.VMEM((cents, frames), bf16),
            pltpu.VMEM((steps, 8, frames), f32),
            jax.ShapeDtypeStruct((8, frames), f32),
            jax.ShapeDtypeStruct((1,), jnp.int32),
        ],
        scratch_shapes=[
            pltpu.VMEM((blocks * ROWS, width), bf16),
            pltpu.VMEM((blocks * ROWS, LANES), f32),
            pltpu.VMEM((blocks * ROWS, LANES), f32),
        ],
        compiler_params=pltpu.CompilerParams(vmem_limit_bytes=12 << 20),
        name="scores",
    )(held, *parts)

    def merge(a, b):
        top = jnp.maximum(a[0:1], b[0:1])
        tot = a[1:2] * jnp.exp2((a[0:1] - top) * k) + b[1:2] * jnp.exp2((b[0:1] - top) * k)
        return jnp.concatenate([top, tot, jnp.zeros_like(a[2:])], axis=0)

    for other in exchange(stats, "cent", cent):
        stats = merge(stats, other)
    all_stats = [stats] + exchange(stats, "section", section)

    return pl.pallas_call(
        functools.partial(refresh_body, k, cb_b, batch),
        in_specs=[VMEM] * 4 + [SMEM] + [VMEM] * len(all_stats),
        out_specs=pl.BlockSpec(memory_space=pl.ANY),
        out_shape=jax.ShapeDtypeStruct((cents, width), f32),
        scratch_shapes=[pltpu.VMEM((2, cb_b, width), f32), pltpu.SemaphoreType.DMA((2,))],
        compiler_params=pltpu.CompilerParams(vmem_limit_bytes=8 << 20),
        name="refresh",
    )(held, frame_rows, e, mb, total, *all_stats)


def general(latents, valid_mask, centroids):
    width = centroids.shape[1]
    frame_rows = lax.all_gather(latents[:VMAX], ("section", "cent"), axis=0, tiled=True)
    frame_flags = lax.all_gather(valid_mask[:VMAX], ("section", "cent"), axis=0, tiled=True)
    scores = lax.dot_general(
        frame_rows,
        centroids.astype(bf16),
        (((1,), (1,)), ((), ())),
        preferred_element_type=f32,
    ) * (3.0 / math.sqrt(width))
    row_max = lax.pmax(jnp.max(scores, axis=1), ("section", "cent"))
    row_total = lax.psum(jnp.sum(jnp.exp(scores - row_max[:, None]), axis=1), ("section", "cent"))
    weights = (
        frame_flags.astype(f32)[:, None] * jnp.exp(scores - row_max[:, None]) / row_total[:, None]
    ).astype(bf16)
    sums = lax.dot_general(
        weights, frame_rows, (((0,), (0,)), ((), ())), preferred_element_type=f32
    )
    soft = jnp.sum(weights, axis=0, dtype=f32)
    sums, soft = lax.psum((sums, soft), "grp")
    return (sums + prior_weight * centroids) / (soft + prior_weight)[:, None]


def solution(mesh):
    sizes = dict(mesh.shape)
    blocks = sizes["section"] * sizes["grp"] * sizes["cent"]

    def per_device(latents, valid_mask, centroids):
        cents, width = centroids.shape
        powers = all(n & (n - 1) == 0 for n in sizes.values())
        folds = (VMAX - ROWS) * width == ROWS * LANES
        if powers and folds and blocks <= 32 and cents % 512 == 0 and cents <= 8192:
            return fast(sizes, latents, valid_mask, centroids)
        return general(latents, valid_mask, centroids)

    return jax.shard_map(
        per_device,
        mesh=mesh,
        in_specs=(
            P(("section", "grp", "cent"), None),
            P(("section", "grp", "cent")),
            P(("section", "cent"), None),
        ),
        out_specs=P(("section", "cent"), None),
        check_vma=False,
    )
```

```python
import functools
import math

import jax
import jax.numpy as jnp
from jax import lax
from jax.experimental import pallas as pl
from jax.experimental.pallas import tpu as pltpu
from jax.sharding import PartitionSpec as P

VMAX = 18
LANES = 128
SCOPE = 9 << 20
ROWS = 16
f32, bf16 = jnp.float32, jnp.bfloat16

prior_weight = 0.05


def pack_body(axes, lat_ref, mask_ref, out_ref):
    width = lat_ref.shape[1]
    rows = lat_ref[...].astype(f32)
    fold = width // LANES
    pieces = [
        rows[r : r + 1, j * LANES : (j + 1) * LANES] for r in range(ROWS, VMAX) for j in range(fold)
    ]
    count = jnp.sum(mask_ref[...].astype(f32), axis=1, keepdims=True)
    block = jnp.int32(0)
    for name, size in axes:
        block = block * size + lax.axis_index(name)
    lane = lax.broadcasted_iota(jnp.int32, (ROWS, LANES), 1)
    tail = jnp.where(lane == 0, count, jnp.where(lane == 1, block.astype(f32), 0.0))
    out_ref[:, :width] = rows[:ROWS].astype(bf16)
    out_ref[:, width : width + LANES] = jnp.concatenate(pieces, axis=0).astype(bf16)
    out_ref[:, width + LANES :] = tail.astype(bf16)


def by_size(total, plans, run):
    for i, (size, *plan) in enumerate(plans):
        over = total > (plans[i - 1][0] if i else -1)
        within = total <= size if i + 1 < len(plans) else True
        pl.when(jnp.logical_and(over, within))(functools.partial(run, size, *plan))


def stack_body(*refs):
    for i, ref in enumerate(refs[:-1]):
        refs[-1][i] = ref[...]


def load_body(pieces, which, _, c_hbm, *refs):
    *c_refs, sem = refs[-pieces - 1 :]
    piece = c_refs[0].shape[0]
    copies = [
        pltpu.make_async_copy(c_hbm.at[pl.ds(i * piece, piece), :], c_refs[i], sem.at[i])
        for i in which
    ]
    for copy in copies:
        copy.start()
    for copy in copies:
        copy.wait()


def order_body(parts, *refs):
    packed, (fr_ref, n_ref, all_ref, ext_ref, meta_ref) = refs[:parts], refs[parts:]
    frames, width = fr_ref.shape

    at = 0
    for part in packed:
        for i in range(part.shape[0]):
            all_ref[at : at + ROWS, :] = part[i, :, :width]
            ext_ref[at : at + ROWS, :] = part[i, :, width : width + LANES].astype(f32)
            meta_ref[at : at + ROWS, :] = part[i, :, width + LANES :].astype(f32)
            at += ROWS
    blocks = at // ROWS
    meta = meta_ref[pl.ds(0, blocks, stride=ROWS), :]
    count, number = meta[:, 0:1], meta[:, 1:2]
    total = jnp.sum(count)
    n_ref[0] = total.astype(jnp.int32)

    def place(rows, block_of, row_of):
        block = lax.broadcasted_iota(jnp.int32, (blocks, rows), 0)
        r = lax.broadcasted_iota(jnp.int32, (blocks, rows), 1)
        mine = block == block_of(r)
        length = jnp.sum(jnp.where(mine, count, 0.0), axis=0, keepdims=True)
        own = jnp.sum(jnp.where(mine, number, 0.0), axis=0, keepdims=True)
        before = jnp.sum(jnp.where(number < own, count, 0.0), axis=0, keepdims=True)
        row = row_of(lax.broadcasted_iota(jnp.int32, (1, rows), 1)).astype(f32)
        return jnp.where(row < length, before + row, -1.0)

    def one_hot(to, start, rows):
        p = lax.broadcasted_iota(jnp.int32, (rows, to.shape[1]), 0) + start
        return jnp.where(p.astype(f32) == to, 1.0, 0.0).astype(bf16)

    extra = VMAX - ROWS
    fold = width // LANES
    main_to = place(at, lambda r: r // ROWS, lambda r: r % ROWS)
    extra_to = place(extra * blocks, lambda r: r % blocks, lambda r: ROWS + r // blocks)
    extra_rows = jnp.concatenate(
        [
            jnp.concatenate(
                [ext_ref[pl.ds(r * fold + j, blocks, stride=ROWS), :] for j in range(fold)], axis=1
            )
            for r in range(extra)
        ],
        axis=0,
    ).astype(bf16)
    chunk = LANES
    for p in range(0, frames, chunk):
        main, ext = one_hot(main_to, p, chunk), one_hot(extra_to, p, chunk)
        ordered = jnp.dot(main, all_ref[...], preferred_element_type=f32)
        ordered += jnp.dot(ext, extra_rows, preferred_element_type=f32)
        fr_ref[p : p + chunk, :] = ordered.astype(bf16)


def scores_body(k, plans, pieces, *refs):
    c_refs, refs = refs[:pieces], refs[pieces:]
    (fr_ref, n_ref), refs = refs[:2], refs[2:]
    e_refs, (mb_ref, st_ref) = refs[:pieces], refs[pieces:]
    piece = c_refs[0].shape[0]
    unit = piece * pieces // mb_ref.shape[0]

    def run(size, cb):
        def block(i, b, carry):
            top, tot = carry
            rows = pl.ds(pl.multiple_of(b * cb, cb), cb)
            raw = lax.dot_general(
                c_refs[i][rows, :].astype(bf16),
                fr_ref[:size, :],
                (((1,), (1,)), ((), ())),
                preferred_element_type=f32,
            )
            m = jnp.max(raw, axis=0, keepdims=True)
            e = jnp.exp2((raw - m) * k)
            e_refs[i][rows, :size] = e.astype(bf16)
            for j in range(cb // unit):
                at = (i * piece + b * cb) // unit + j
                mb_ref[at, :, :size] = jnp.broadcast_to(m, (8, size))
            new = jnp.maximum(top, m)
            part = jnp.sum(e, axis=0, keepdims=True)
            tot = tot * jnp.exp2((top - new) * k) + part * jnp.exp2((m - new) * k)
            return new, tot

        carry = jnp.full((1, size), -1e30, f32), jnp.zeros((1, size), f32)
        for i in range(pieces):
            carry = lax.fori_loop(0, piece // cb, functools.partial(block, i), carry)
        st_ref[...] = jnp.zeros_like(st_ref)
        st_ref[0:1, :size] = carry[0]
        st_ref[1:2, :size] = carry[1]

    by_size(n_ref[0], plans, run)


def refresh_body(k, plans, pieces, *refs):
    c_refs, refs = refs[:pieces], refs[pieces:]
    e_refs, refs = refs[:pieces], refs[pieces:]
    (fr_ref, mb_ref, n_ref), refs = refs[:3], refs[3:]
    stats, refs = refs[: -pieces - 2], refs[-pieces - 2 :]
    d_refs, (o_ref, sem) = refs[:pieces], refs[pieces:]
    piece, width = c_refs[0].shape
    total = n_ref[0]

    def run(size, cb, unroll):
        per = mb_ref.shape[0] * cb // (piece * pieces)
        top = functools.reduce(jnp.maximum, [s[0:1, :size] for s in stats])
        denom = functools.reduce(
            jnp.add, [s[1:2, :size] * jnp.exp2((s[0:1, :size] - top) * k) for s in stats]
        )
        valid = lax.broadcasted_iota(jnp.int32, (1, size), 1) < total
        keep = jnp.where(valid, 1.0 / denom, 0.0)

        def put(i, rows, to):
            return pltpu.make_async_copy(d_refs[i].at[rows, :], o_ref.at[to, :], sem.at[i])

        def block(i, b, _):
            rows = pl.ds(pl.multiple_of(b * cb, cb), cb)
            to = pl.ds(pl.multiple_of(i * piece + b * cb, cb), cb)
            scale = jnp.exp2((mb_ref[(i * (piece // cb) + b) * per, 0:1, :size] - top) * k) * keep
            w = (e_refs[i][rows, :size].astype(f32) * scale).astype(bf16)
            soft = jnp.sum(w.astype(f32), axis=1, keepdims=True)
            sums = jnp.dot(w, fr_ref[:size, :], preferred_element_type=f32)
            d_refs[i][rows, :] = (sums + prior_weight * c_refs[i][rows, :]) * (
                1.0 / (soft + prior_weight)
            )
            put(i, rows, to).start()
            return 0

        for i in range(pieces):
            lax.fori_loop(0, piece // cb, functools.partial(block, i), 0, unroll=unroll)
        for i in range(pieces):
            put(i, pl.ds(0, piece), pl.ds(i * piece, piece)).wait()

    by_size(total, plans, run)


VMEM = pl.BlockSpec(memory_space=pltpu.VMEM)
SMEM = pl.BlockSpec(memory_space=pltpu.SMEM)
HBM = pl.BlockSpec(memory_space=pltpu.HBM)


def exchange(x, axis, size):
    return [lax.ppermute(x, axis, [(i, i ^ d) for i in range(size)]) for d in range(1, size)]


def fast(sizes, latents, valid_mask, centroids):
    cents, width = centroids.shape
    k = 3.0 / math.sqrt(width) * math.log2(math.e)
    section, grp, cent = sizes["section"], sizes["grp"], sizes["cent"]
    blocks = section * grp * cent
    frames = -(-blocks * VMAX // LANES) * LANES
    small = frames * 4 // 5 // LANES * LANES
    cb = 512
    pieces = 4
    piece = cents // pieces

    packed = pl.pallas_call(
        functools.partial(pack_body, (("section", section), ("grp", grp), ("cent", cent))),
        in_specs=[VMEM, VMEM],
        out_specs=VMEM,
        out_shape=jax.ShapeDtypeStruct((ROWS, width + 2 * LANES), bf16),
        compiler_params=pltpu.CompilerParams(vmem_limit_bytes=SCOPE),
        name="pack",
    )(latents, valid_mask[None, :])

    def load(which, after, *held):
        return pl.pallas_call(
            functools.partial(load_body, pieces, which),
            in_specs=[HBM, HBM] + [VMEM] * len(held),
            out_specs=[VMEM] * pieces,
            out_shape=[pltpu.VMEM((piece, width), f32)] * pieces,
            input_output_aliases={2 + i: i for i in range(len(held))},
            scratch_shapes=[pltpu.SemaphoreType.DMA((pieces,))],
            compiler_params=pltpu.CompilerParams(vmem_limit_bytes=SCOPE),
            cost_estimate=pl.CostEstimate(
                flops=0, transcendentals=0, bytes_accessed=cents * width * 4
            ),
            name="load",
        )(after, pltpu.with_memory_space_constraint(centroids, pltpu.HBM), *held)

    others = exchange(packed, "grp", grp)
    column = pl.pallas_call(
        stack_body,
        in_specs=[VMEM] * grp,
        out_specs=VMEM,
        out_shape=jax.ShapeDtypeStruct((grp, *packed.shape), bf16),
        compiler_params=pltpu.CompilerParams(vmem_limit_bytes=SCOPE),
        name="stack",
    )(packed, *others)
    held = load(range(pieces), column)
    others, held = lax.optimization_barrier((exchange(column, "section", section), held))
    half = [column] + others
    parts = half + [x for h in half for x in exchange(h, "cent", cent)]

    frame_rows, total = pl.pallas_call(
        functools.partial(order_body, len(parts)),
        in_specs=[VMEM] * len(parts),
        out_specs=[VMEM, SMEM],
        out_shape=[
            pltpu.VMEM((frames, width), bf16),
            jax.ShapeDtypeStruct((1,), jnp.int32),
        ],
        scratch_shapes=[
            pltpu.VMEM((blocks * ROWS, width), bf16),
            pltpu.VMEM((blocks * ROWS, LANES), f32),
            pltpu.VMEM((blocks * ROWS, LANES), f32),
        ],
        compiler_params=pltpu.CompilerParams(vmem_limit_bytes=SCOPE),
        name="order",
    )(*parts)

    *e, mb, stats = pl.pallas_call(
        functools.partial(scores_body, k, ((small, cb), (frames, cb // 2)), pieces),
        in_specs=[VMEM] * (pieces + 1) + [SMEM],
        out_specs=[VMEM] * (pieces + 2),
        out_shape=[pltpu.VMEM((piece, frames), bf16)] * pieces
        + [
            pltpu.VMEM((2 * cents // cb, 8, frames), f32),
            jax.ShapeDtypeStruct((8, frames), f32),
        ],
        compiler_params=pltpu.CompilerParams(vmem_limit_bytes=SCOPE),
        name="scores",
    )(*held, frame_rows, total)

    def merge(a, b):
        top = jnp.maximum(a[0:1], b[0:1])
        tot = a[1:2] * jnp.exp2((a[0:1] - top) * k) + b[1:2] * jnp.exp2((b[0:1] - top) * k)
        return jnp.concatenate([top, tot, jnp.zeros_like(a[2:])], axis=0)

    for other in exchange(stats, "cent", cent):
        stats = merge(stats, other)
    all_stats = [stats] + exchange(stats, "section", section)

    return pl.pallas_call(
        functools.partial(refresh_body, k, ((small, cb, 2), (frames, cb // 2, 1)), pieces),
        in_specs=[VMEM] * (2 * pieces + 2) + [SMEM] + [VMEM] * len(all_stats),
        out_specs=[VMEM] * pieces + [HBM],
        out_shape=[pltpu.VMEM((piece, width), f32)] * pieces
        + [jax.ShapeDtypeStruct((cents, width), f32)],
        input_output_aliases={i: i for i in range(pieces)},
        scratch_shapes=[pltpu.SemaphoreType.DMA((pieces,))],
        compiler_params=pltpu.CompilerParams(vmem_limit_bytes=SCOPE),
        name="refresh",
    )(*held, *e, frame_rows, mb, total, *all_stats)[-1]


def general(latents, valid_mask, centroids):
    width = centroids.shape[1]
    frame_rows = lax.all_gather(latents[:VMAX], ("section", "cent"), axis=0, tiled=True)
    frame_flags = lax.all_gather(valid_mask[:VMAX], ("section", "cent"), axis=0, tiled=True)
    scores = lax.dot_general(
        frame_rows,
        centroids.astype(bf16),
        (((1,), (1,)), ((), ())),
        preferred_element_type=f32,
    ) * (3.0 / math.sqrt(width))
    row_max = lax.pmax(jnp.max(scores, axis=1), ("section", "cent"))
    row_total = lax.psum(jnp.sum(jnp.exp(scores - row_max[:, None]), axis=1), ("section", "cent"))
    weights = (
        frame_flags.astype(f32)[:, None] * jnp.exp(scores - row_max[:, None]) / row_total[:, None]
    ).astype(bf16)
    sums = lax.dot_general(
        weights, frame_rows, (((0,), (0,)), ((), ())), preferred_element_type=f32
    )
    soft = jnp.sum(weights, axis=0, dtype=f32)
    sums, soft = lax.psum((sums, soft), "grp")
    return (sums + prior_weight * centroids) / (soft + prior_weight)[:, None]


def solution(mesh):
    sizes = dict(mesh.shape)
    blocks = sizes["section"] * sizes["grp"] * sizes["cent"]

    def per_device(latents, valid_mask, centroids):
        cents, width = centroids.shape
        powers = all(n & (n - 1) == 0 for n in sizes.values())
        folds = (VMAX - ROWS) * width == ROWS * LANES
        if powers and folds and blocks <= 32 and cents % 4096 == 0 and cents <= 8192 and width <= 1024:
            return fast(sizes, latents, valid_mask, centroids)
        return general(latents, valid_mask, centroids)

    return jax.shard_map(
        per_device,
        mesh=mesh,
        in_specs=(
            P(("section", "grp", "cent"), None),
            P(("section", "grp", "cent")),
            P(("section", "cent"), None),
        ),
        out_specs=P(("section", "cent"), None),
        check_vma=False,
    )
```
